128 devices in a mesh: blk: 64 (over z, y, x_hi, core), head: 2 (over x_lo).
Axes of the slice: x: 4 (x_hi: 2, x_lo: 2; x = x_hi * 2 + x_lo), y: 4, z: 4, core: 2. Of those that a mesh axis runs over, the one named last changes fastest.
Arguments:
- queries: bfloat16 [16384, 4096], P(('blk', 'head')), may hold values from -15 to 15
- keys: bfloat16 [16384, 512], P(('blk', 'head')), may hold values from -6 to 6
- values: bfloat16 [16384, 512], P(('blk', 'head')), may hold values from -6 to 6
- span_pos: int32 [128], replicated, may hold values from 0 to 127, as said below
Outputs:
- attended: bfloat16 [16384, 4096], P(('blk', 'head'))
The draws below stay inside these ranges and needn't reach their ends.
Inputs may be any that keep to these rules, and one draw needn't show every extreme that they name: `span_pos`: a permutation of 0 to 127; entries 2 b and 2 b + 1 sum to 127 for every b.
All inputs are finite; a program needn't handle non-finite values.
Results may differ from the reference program's by a relative error of at most 0.0065.
Values may be sent and summed in bfloat16 or wider, within the bound.
No kernel may reach another device: no remote copies, remote signals or barrier semaphores. Data moves between devices by JAX's collectives and lax.ppermute only.
A program may use at most 192 MiB of HBM per device.

```python
import jax
import jax.numpy as jnp
from jax import lax

QUERY_HEADS = 32
KEY_VALUE_HEADS = 4
HEAD_DIMENSION = 128
TOKENS_PER_PART = 128
QUERY_PER_KV = 8
NCH = 128
WINDOW_TOKENS = 16384


def draw_queries(key, part):
    root_random_key = jax.random.fold_in(jax.random.fold_in(key, 11), 0)
    drawn_sample = jnp.clip(jax.random.normal(root_random_key, (WINDOW_TOKENS, QUERY_HEADS, HEAD_DIMENSION), jnp.float32) * 2.5, -15.0, 15.0)
    return jnp.clip(drawn_sample, -15.0, 15.0).reshape(WINDOW_TOKENS, QUERY_HEADS * HEAD_DIMENSION).astype(jnp.bfloat16)


def draw_keys(key, part):
    root_random_key = jax.random.fold_in(jax.random.fold_in(key, 23), 0)
    drawn_sample = jax.random.normal(root_random_key, (WINDOW_TOKENS, KEY_VALUE_HEADS, HEAD_DIMENSION), jnp.float32)
    return jnp.clip(drawn_sample, -6.0, 6.0).reshape(WINDOW_TOKENS, KEY_VALUE_HEADS * HEAD_DIMENSION).astype(jnp.bfloat16)


def draw_span_pos(key, part):
    perm_key, flip_key = jax.random.split(jax.random.fold_in(key, 31))
    low = jax.random.permutation(perm_key, NCH // 2).astype(jnp.int32)
    high = (NCH - 1 - low).astype(jnp.int32)
    flips = jax.random.randint(flip_key, (NCH // 2,), 0, 2)
    first = jnp.where(flips == 1, high, low)
    second = jnp.where(flips == 1, low, high)
    return jnp.stack([first, second], axis=1).reshape(NCH).astype(jnp.int32)


def steps_of(stream_key, shape, cuts, smallest, largest):
    level = 1.0
    for axis_at, parts in cuts:
        draws = jax.random.uniform(jax.random.fold_in(jax.random.fold_in(stream_key, 6), axis_at), (parts,), jnp.float32, smallest / len(cuts), largest / len(cuts))
        level = level * jnp.repeat(jnp.exp(draws), shape[axis_at] // parts).reshape((-1,) + (1,) * (len(shape) - 1 - axis_at))
    return level


def noise(own_key, dims, width, reach, pieces=(), held_as=jnp.bfloat16):
    entries = jax.random.normal(own_key, dims, jnp.float32) * width
    if len(pieces) > 0:
        entries = steps_of(own_key, dims, pieces, -0.22, 0.18) * entries
    return jnp.clip(entries, min=-reach, max=reach).astype(held_as)


def setup_inputs(seed: int = 0) -> dict:
    arg_keys = jax.random.split(jax.random.key(seed), 5)
    queries = draw_queries(jax.random.fold_in(arg_keys[4], 71), 0)
    keys = draw_keys(jax.random.fold_in(arg_keys[4], 71), 0)
    values = noise(arg_keys[2], (WINDOW_TOKENS, KEY_VALUE_HEADS * HEAD_DIMENSION), 1.0, 6.0, ((0, 128),))
    span_pos = draw_span_pos(jax.random.fold_in(arg_keys[4], 71), 0)
    return {"queries": queries, "keys": keys, "values": values, "span_pos": span_pos}


def reference(queries, keys, values, span_pos):
    offsets = jnp.arange(TOKENS_PER_PART, dtype=jnp.int32)
    positions = (span_pos[:, None] * TOKENS_PER_PART + offsets[None, :]).reshape(WINDOW_TOKENS).astype(jnp.int32)
    gathered_keys = keys.reshape(WINDOW_TOKENS, KEY_VALUE_HEADS, HEAD_DIMENSION).astype(jnp.float32)
    gathered_values = values.reshape(WINDOW_TOKENS, KEY_VALUE_HEADS, HEAD_DIMENSION).astype(jnp.float32)
    scale = 1.0 / (HEAD_DIMENSION ** 0.5)

    def one_block(index):
        begin_position = (index * TOKENS_PER_PART).astype(jnp.int32)
        row_values = lax.dynamic_slice_in_dim(queries, begin_position, TOKENS_PER_PART, 0).reshape(TOKENS_PER_PART, KEY_VALUE_HEADS, QUERY_PER_KV, HEAD_DIMENSION).astype(jnp.float32)
        row_pos = lax.dynamic_slice_in_dim(positions, begin_position, TOKENS_PER_PART, 0)
        scores = jnp.einsum('rgqd,kgd->gqrk', row_values, gathered_keys) * scale
        allowed = row_pos[:, None] >= positions[None, :]
        scores = jnp.where(allowed[None, None], scores, -jnp.inf)
        peak = jnp.max(scores, axis=-1, keepdims=True)
        expo = jnp.exp(scores - peak)
        total = jnp.sum(expo, axis=-1)
        weights = expo.astype(jnp.bfloat16).astype(jnp.float32)
        summed = jnp.einsum('gqrk,kgd->gqrd', weights, gathered_values)
        result = summed / total[..., None]
        return jnp.transpose(result, (2, 0, 1, 3)).reshape(TOKENS_PER_PART, QUERY_HEADS * HEAD_DIMENSION).astype(jnp.bfloat16)

    blocks = lax.map(one_block, jnp.arange(WINDOW_TOKENS // TOKENS_PER_PART, dtype=jnp.int32))
    return blocks.reshape(WINDOW_TOKENS, QUERY_HEADS * HEAD_DIMENSION)
```

```python
import functools

import jax
import jax.numpy as jnp
from jax import lax
from jax.experimental import pallas as pl
from jax.experimental.pallas import tpu as pltpu
from jax.sharding import PartitionSpec as P

D = 128
HEADS = 4
GROUP = 8
COLS = GROUP * D
F32 = jnp.float32
BF16 = jnp.bfloat16
FACTOR = 1.4426950408889634 / D**0.5
LIMIT = 2.0**100
AXES = ("blk", "head")
TILE = 8


def xbits(e):
    return ((e >> 1) << 2) | (e & 1)


def zbits(e):
    return e << 5


def ybits(e):
    return e << 3


CORE = 2


def swap(array, mask):
    return lax.ppermute(array, AXES, [(i, i ^ mask) for i in range(128)])


def nt(a, b):
    return lax.dot_general(a, b, (((1,), (1,)), ((), ())), preferred_element_type=F32)


def nn(a, b):
    return lax.dot_general(a, b, (((1,), (0,)), ((), ())), preferred_element_type=F32)


def heads_of(q_ref):
    return jnp.concatenate([q_ref[:, h * D : (h + 1) * D] for h in range(GROUP)], axis=0)


def fold(p):
    return jnp.sum(p.reshape(p.shape[0] // 8, 8, p.shape[1]), axis=0)


def causal():
    row = lax.broadcasted_iota(jnp.int32, (D, COLS), 0)
    col = lax.broadcasted_iota(jnp.int32, (D, COLS), 1) % D
    return row <= col


def kernel(
    first,
    last,
    slots,
    chunk_arrays,
    rank_ref,
    count_ref,
    all_pos_ref,
    q_pos_ref,
    *refs,
):
    refs = list(refs)
    q_refs = [refs.pop(0) for _ in range(4)]
    own = refs.pop(0) if first else None
    if not first:
        acc_in, l_in, m_in = refs.pop(0), refs.pop(0), refs.pop(0)
    n_all = len(refs) - (11 if last else 7)
    arrays = [refs.pop(0) for _ in range(n_all)]
    here = arrays[-chunk_arrays:]
    if last:
        o_ref = refs.pop(0)
        acc, l_sum, shift = refs.pop(0), refs.pop(0), refs.pop(0)
    else:
        acc, l_sum, shift = refs.pop(0), refs.pop(0), refs.pop(0)
    keys, values, sem_k, sem_v = refs[:4]

    at = 0
    for array in here:
        for i in range(array.shape[0]):
            base = pl.multiple_of(rank_ref[at] * D, D)
            pltpu.make_async_copy(array.at[i, 0], keys.at[pl.ds(base, D), :], sem_k).start()
            pltpu.make_async_copy(array.at[i, 1], values.at[:, pl.ds(base, D)], sem_v).start()
            at += 1

    if first:
        for b in range(4):
            s = nt(own[b, 0], heads_of(q_refs[b])) * FACTOR
            s = jnp.where(causal(), s, -jnp.inf)
            m = jnp.max(s, axis=0, keepdims=True)
            p = jnp.exp2(s - m)
            shift[b] = jnp.broadcast_to(m, (8, COLS))
            l_sum[b] = fold(p)
            acc[b] = nn(own[b, 1], p.astype(BF16))
    else:
        acc[...] = acc_in[...]
        l_sum[...] = l_in[...]
        shift[...] = m_in[...]

    pltpu.make_async_copy(keys, keys, sem_k).wait()
    pltpu.make_async_copy(values, values, sem_v).wait()

    def tile(b, base, blocks, limit):
        k = keys[pl.ds(base, blocks * D), :]
        vt = values[:, pl.ds(base, blocks * D)]
        s = nt(k, heads_of(q_refs[b])) * FACTOR - shift[b, 0:1, :]
        p = jnp.exp2(s)
        if limit is not None:
            row = lax.broadcasted_iota(jnp.int32, (blocks * D, COLS), 0)
            p = jnp.where(row < limit, p, 0.0)
        l_sum[b] += fold(p)
        acc[b] += nn(vt, p.astype(BF16))

    for b in range(4):
        count = count_ref[b]
        whole = count // TILE

        def step(j, _, b=b):
            tile(b, pl.multiple_of(j * (TILE * D), TILE * D), TILE, None)
            return 0

        lax.fori_loop(0, whole, step, 0)
        rest = count - whole * TILE
        half = rest >= 4

        @pl.when(half)
        def _(b=b, whole=whole):
            tile(b, pl.multiple_of(whole * (TILE * D), 4 * D), 4, None)

        done = whole * TILE + jnp.where(half, 4, 0)

        @pl.when(count > done)
        def _(b=b, done=done, count=count):
            tile(b, pl.multiple_of(done * D, 4 * D), 4, (count - done) * D)

    if not last:
        return
    l_ref, k_one, v_one = refs[4:7]
    for b in range(4):
        total = jnp.sum(l_sum[b], axis=0, keepdims=True)
        bad = jnp.max(jnp.where(total < LIMIT, 0.0, 1.0)) > 0.0

        @pl.when(bad)
        def _(b=b):
            q_pos = q_pos_ref[b]
            l_ref[...] = jnp.zeros_like(l_ref)
            acc[b] = jnp.zeros((D, COLS), F32)
            shift[b] = jnp.full((8, COLS), -jnp.inf, F32)
            at = 0
            for array in arrays:

                def one(i, _, array=array, at=at):
                    k_pos = all_pos_ref[at + i]

                    @pl.when(k_pos <= q_pos)
                    def _():
                        pltpu.sync_copy(array.at[i, 0], k_one)
                        pltpu.sync_copy(array.at[i, 1], v_one)
                        s = nt(k_one[...], heads_of(q_refs[b])) * FACTOR
                        row = lax.broadcasted_iota(jnp.int32, (D, COLS), 0) + k_pos * D
                        col = lax.broadcasted_iota(jnp.int32, (D, COLS), 1) % D + q_pos * D
                        s = jnp.where(row <= col, s, -jnp.inf)
                        old = shift[b, 0:1, :]
                        m = jnp.maximum(old, jnp.max(s, axis=0, keepdims=True))
                        safe = jnp.where(m == -jnp.inf, 0.0, m)
                        scale = jnp.exp2(old - safe)
                        p = jnp.exp2(s - safe)
                        shift[b] = jnp.broadcast_to(m, (8, COLS))
                        l_ref[...] = l_ref[...] * scale + fold(p)
                        acc[b] = acc[b] * scale + nn(v_one[...], p.astype(BF16))

                    return 0

                lax.fori_loop(0, array.shape[0], one, 0)
                at += array.shape[0]
            l_sum[b] = l_ref[...]

        total = jnp.sum(l_sum[b], axis=0, keepdims=True)
        out = acc[b] / total
        for h in range(GROUP):
            o_ref[b, :, h * D : (h + 1) * D] = out[:, h * D : (h + 1) * D].T.astype(BF16)


def attend(rank, count, all_pos, q_pos, q_parts, own, state, before, here, last):
    first = state is None
    slots = sum(a.shape[0] for a in here)
    vmem = pl.BlockSpec(memory_space=pltpu.VMEM)
    smem = pl.BlockSpec(memory_space=pltpu.SMEM)
    hbm = pl.BlockSpec(memory_space=pl.ANY)
    arrays = (list(before) if last else []) + list(here)
    operands = [rank, count, all_pos, q_pos, *q_parts]
    specs = [smem] * 4 + [vmem] * 4
    if first:
        operands.append(own)
        specs.append(vmem)
    else:
        operands += list(state)
        specs += [vmem] * 3
    operands += arrays
    specs += [hbm] * len(arrays)
    state_shapes = [
        jax.ShapeDtypeStruct((4, D, COLS), F32),
        jax.ShapeDtypeStruct((4, 8, COLS), F32),
        jax.ShapeDtypeStruct((4, 8, COLS), F32),
    ]
    scratch = [
        pltpu.VMEM((slots * D, D), BF16),
        pltpu.VMEM((D, slots * D), BF16),
        pltpu.SemaphoreType.DMA,
        pltpu.SemaphoreType.DMA,
    ]
    if last:
        out_shape = jax.ShapeDtypeStruct((4, D, COLS), BF16)
        out_specs = vmem
        scratch = [pltpu.VMEM(s.shape, s.dtype) for s in state_shapes] + scratch
        scratch += [pltpu.VMEM((8, COLS), F32), pltpu.VMEM((D, D), BF16), pltpu.VMEM((D, D), BF16)]
    else:
        out_shape = state_shapes
        out_specs = [vmem] * 3
    units = slots * 2
    return pl.pallas_call(
        functools.partial(kernel, first, last, slots, len(here)),
        out_shape=out_shape,
        in_specs=specs,
        out_specs=out_specs,
        scratch_shapes=scratch,
        compiler_params=pltpu.CompilerParams(vmem_limit_bytes=56 << 20),
        cost_estimate=pl.CostEstimate(
            flops=units * 4 * D * D * COLS, bytes_accessed=slots * D * D * 4, transcendentals=0
        ),
    )(*operands)


def body(queries, keys, values, span_pos):
    flat = lax.axis_index("blk") * 2 + lax.axis_index("head")
    x = ((flat >> 2) & 1) * 2 + (flat & 1)

    by_head = jnp.stack(
        [
            keys.reshape(D, HEADS, D).transpose(1, 0, 2),
            values.reshape(D, HEADS, D).transpose(1, 2, 0),
        ],
        axis=1,
    )

    def head_part(e):
        return lax.dynamic_index_in_dim(by_head, x ^ e, 0, keepdims=True)

    def query_part(e):
        return lax.dynamic_slice_in_dim(queries, (x ^ e) * COLS, COLS, 1)

    shard = [head_part(0)] + [swap(head_part(e), xbits(e)) for e in (1, 2, 3)]
    q_parts = [query_part(0)] + [swap(query_part(e), xbits(e)) for e in (1, 2, 3)]
    own = jnp.concatenate(shard, 0)
    half_a, half_b = own[:2], own[2:]
    a4 = jnp.concatenate([half_a] + [swap(half_a, zbits(e)) for e in (1, 2, 3)], 0)
    b4 = jnp.concatenate([half_b] + [swap(half_b, ybits(e)) for e in (1, 2, 3)], 0)
    near = [a4, b4]
    a_masks = [zbits(e) | xbits(i) for e in range(4) for i in (0, 1)]
    b_masks = [ybits(e) | xbits(i) for e in range(4) for i in (2, 3)]
    sets = [near]
    masks = [[a_masks, b_masks]]
    for shifts in ((1, 3), (2,)):
        sets.append([])
        masks.append([])
        for e in shifts:
            sets[-1] += [swap(a4, ybits(e)), swap(b4, zbits(e))]
            masks[-1] += [[m ^ ybits(e) for m in a_masks], [m ^ zbits(e) for m in b_masks]]
    sets = [s + [swap(a, CORE) for a in s] for s in sets]
    masks = [[m for part in ms for m in part] + [m ^ CORE for part in ms for m in part] for ms in masks]

    chunks = [[a for s in sets for a in s]]
    chunk_masks = [[m for ms in masks for m in ms]]

    order = jnp.array([m for ms in chunk_masks for m in ms], jnp.int32)
    all_pos = span_pos[flat ^ order]
    q_pos = span_pos[flat ^ jnp.array([xbits(e) for e in range(4)], jnp.int32)]
    state = None
    before = []
    at = 0
    for i, chunk in enumerate(chunks):
        n = len(chunk_masks[i])
        pos = all_pos[at : at + n]
        at += n
        rank = jnp.sum((pos[None, :] < pos[:, None]).astype(jnp.int32), axis=1)
        count = jnp.sum((pos[None, :] < q_pos[:, None]).astype(jnp.int32), axis=1)
        state = attend(
            rank, count, all_pos, q_pos, q_parts, own, state, before, chunk, i == len(chunks) - 1
        )
        before += chunk
    out = state
    pieces = [out[0]] + [swap(out[e], xbits(e)) for e in (1, 2, 3)]
    result = jnp.zeros((D, HEADS * COLS), BF16)
    for e in range(4):
        result = lax.dynamic_update_slice(result, pieces[e], (0, (x ^ e) * COLS))
    return result


def solution(mesh):
    return jax.shard_map(
        body,
        mesh=mesh,
        in_specs=(P(AXES, None), P(AXES, None), P(AXES, None), P()),
        out_specs=P(AXES, None),
        check_vma=False,
    )
```

```python
import functools

import jax
import jax.numpy as jnp
from jax import lax
from jax.experimental import pallas as pl
from jax.experimental.pallas import tpu as pltpu
from jax.sharding import PartitionSpec as P

D = 128
HEADS = 4
GROUP = 8
COLS = GROUP * D
F32 = jnp.float32
BF16 = jnp.bfloat16
FACTOR = 1.4426950408889634 / D**0.5
SMALL = 4
LIMIT = 2.0**100
ONES = 16
ROWS = D + ONES
VMEM_LIMIT = 40 << 20
AXES = ("blk", "head")
TILE = 8


def xbits(e):
    return ((e >> 1) << 2) | (e & 1)


def zbits(e):
    return e << 5


def ybits(e):
    return e << 3


CORE = 2


def swap(array, mask):
    return lax.ppermute(array, AXES, [(i, i ^ mask) for i in range(128)])


def nt(a, b):
    return lax.dot_general(a, b, (((1,), (1,)), ((), ())), preferred_element_type=F32)


def nn(a, b):
    return lax.dot_general(a, b, (((1,), (0,)), ((), ())), preferred_element_type=F32)


def pick(choices, i):
    chosen = jnp.int32(choices[-1])
    for at, choice in reversed(list(enumerate(choices[:-1]))):
        chosen = jnp.where(i == at, choice, chosen)
    return chosen


def causal():
    row = lax.broadcasted_iota(jnp.int32, (D, COLS), 0)
    col = lax.broadcasted_iota(jnp.int32, (D, COLS), 1) % D
    return row <= col


def kernel(first, blocks, chunk_arrays, rank_ref, count_ref, all_pos_ref, q_pos_ref, *refs):
    refs = list(refs)
    q_refs = [refs.pop(0) for _ in range(4)]
    own = refs.pop(0) if first else None
    if not first:
        acc_in, shift_in = refs.pop(0), refs.pop(0)
    n_out = len(blocks) or 2
    arrays = [refs.pop(0) for _ in range(len(refs) - n_out - (9 if blocks else 5))]
    here = arrays[-chunk_arrays:]
    outs = [refs.pop(0) for _ in range(n_out)]
    keys, values, q_all, sem_k, sem_v = [refs.pop(0) for _ in range(5)]
    acc, shift = (refs.pop(0), refs.pop(0)) if blocks else outs
    todo = blocks or (0, 1, 2, 3)

    at = 0
    for array in here:

        def place(i, _, array=array, at=at):
            base = pl.multiple_of(rank_ref[at + i] * D, D)
            pltpu.make_async_copy(array.at[i, 0], keys.at[pl.ds(base, D), :], sem_k).start()
            pltpu.make_async_copy(
                array.at[i, 1], values.at[0:D, pl.ds(base, D)], sem_v
            ).start()
            return 0

        lax.fori_loop(0, array.shape[0], place, 0, unroll=True)
        at += array.shape[0]

    values[D:, :] = jnp.ones((ONES, values.shape[1]), BF16)
    for b in todo:
        for h in range(GROUP):
            q_all[b, h * D : (h + 1) * D, :] = q_refs[b][:, h * D : (h + 1) * D]

    if first:

        def diagonal(b, _):
            s = nt(own[b, 0], q_all[b]) * FACTOR
            s = jnp.where(causal(), s, -jnp.inf)
            m = jnp.max(s, axis=0, keepdims=True)
            p = jnp.exp2(s - m).astype(BF16)
            shift[b] = jnp.broadcast_to(m, (8, COLS))
            acc[b] = nn(jnp.concatenate([own[b, 1], jnp.ones((ONES, D), BF16)], axis=0), p)
            return 0

        lax.fori_loop(0, 4, diagonal, 0)
    else:
        for b in todo:
            acc[b] = acc_in[b]
            shift[b] = shift_in[b]

    pltpu.make_async_copy(keys, keys, sem_k).wait()
    pltpu.make_async_copy(values.at[0:D, :], values.at[0:D, :], sem_v).wait()

    def tile(b, at, width):
        size = width * D
        base = pl.multiple_of(at * D, SMALL * D)
        s = nt(keys[pl.ds(base, size), :], q_all[b])
        p = jnp.exp2(s * FACTOR - shift[b, 0:1, :]).astype(BF16)
        col = lax.broadcasted_iota(jnp.int32, (ROWS, size), 1)
        v = values[:, pl.ds(base, size)]
        v = jnp.where(col < (count_ref[b] - at) * D, v, jnp.zeros_like(v))
        acc[b] += nn(v, p)

    def block(b, _):
        count = count_ref[b]
        large = (count + TILE - 1 - SMALL) // TILE

        def step(j, _):
            tile(b, j * TILE, TILE)
            return 0

        lax.fori_loop(0, large, step, 0)
        pl.when(count > large * TILE)(lambda: tile(b, large * TILE, SMALL))
        return 0

    lax.fori_loop(0, len(todo), lambda i, c: block(pick(todo, i), c), 0)

    if not blocks:
        return
    k_one, v_one = refs

    def redo(b):
        q_pos = q_pos_ref[b]
        acc[b] = jnp.zeros((ROWS, COLS), F32)
        shift[b] = jnp.full((8, COLS), -jnp.inf, F32)

        def one(i, _):
            k_pos = all_pos_ref[i]

            @pl.when(k_pos <= q_pos)
            def _():
                at = 0
                for array in arrays:
                    n = array.shape[0]

                    @pl.when((i >= at) & (i < at + n))
                    def _(array=array, at=at):
                        pltpu.sync_copy(array.at[i - at, 0], k_one)
                        pltpu.sync_copy(array.at[i - at, 1], v_one.at[0:D, :])

                    at += n
                s = nt(k_one[...], q_all[b]) * FACTOR
                row = lax.broadcasted_iota(jnp.int32, (D, COLS), 0) + k_pos * D
                col = lax.broadcasted_iota(jnp.int32, (D, COLS), 1) % D + q_pos * D
                s = jnp.where(row <= col, s, -jnp.inf)
                old = shift[b, 0:1, :]
                m = jnp.maximum(old, jnp.max(s, axis=0, keepdims=True))
                safe = jnp.where(m == -jnp.inf, 0.0, m)
                p = jnp.exp2(s - safe).astype(BF16)
                shift[b] = jnp.broadcast_to(m, (8, COLS))
                acc[b] = acc[b] * jnp.exp2(old - safe) + nn(v_one[...], p)

            return 0

        lax.fori_loop(0, all_pos_ref.shape[0], one, 0)

    v_one[D:, :] = jnp.ones((ONES, D), BF16)

    def check(b, _):
        total = acc[b, D : D + 1, :]
        bad = jnp.max(jnp.where(total < LIMIT, 0.0, 1.0)) > 0.0
        pl.when(bad)(lambda: redo(b))
        return 0

    lax.fori_loop(0, len(todo), lambda i, c: check(pick(todo, i), c), 0)
    for o_ref, b in zip(outs, blocks):
        out = acc[b, :D, :] / acc[b, D : D + 1, :]
        for h in range(GROUP):
            o_ref[:, h * D : (h + 1) * D] = out[:, h * D : (h + 1) * D].T.astype(BF16)


def attend(rank, count, all_pos, q_pos, q_parts, own, state, before, here, blocks):
    first = state is None
    slots = sum(a.shape[0] for a in here)
    vmem = pl.BlockSpec(memory_space=pltpu.VMEM)
    smem = pl.BlockSpec(memory_space=pltpu.SMEM)
    hbm = pl.BlockSpec(memory_space=pl.ANY)
    arrays = (list(before) if blocks else []) + list(here)
    operands = [rank, count, all_pos, q_pos, *q_parts]
    specs = [smem] * 4 + [vmem] * 4
    operands += [own] if first else list(state)
    specs += [vmem] * (1 if first else 2)
    operands += arrays
    specs += [hbm] * len(arrays)
    scratch = [
        pltpu.VMEM((slots * D, D), BF16),
        pltpu.VMEM((ROWS, slots * D), BF16),
        pltpu.VMEM((4, COLS, D), BF16),
        pltpu.SemaphoreType.DMA,
        pltpu.SemaphoreType.DMA,
    ]
    if blocks:
        out_shape = [jax.ShapeDtypeStruct((D, COLS), BF16) for _ in blocks]
        scratch += [pltpu.VMEM((4, ROWS, COLS), F32), pltpu.VMEM((4, 8, COLS), F32)]
        scratch += [pltpu.VMEM((D, D), BF16), pltpu.VMEM((ROWS, D), BF16)]
    else:
        out_shape = [
            jax.ShapeDtypeStruct((4, ROWS, COLS), F32),
            jax.ShapeDtypeStruct((4, 8, COLS), F32),
        ]
    share = len(blocks) / 4 if blocks else 1
    return pl.pallas_call(
        functools.partial(kernel, first, tuple(blocks), len(here)),
        out_shape=out_shape,
        in_specs=specs,
        out_specs=[vmem] * len(out_shape),
        scratch_shapes=scratch,
        compiler_params=pltpu.CompilerParams(vmem_limit_bytes=VMEM_LIMIT),
        cost_estimate=pl.CostEstimate(
            flops=int(slots * 2 * share) * 8 * D * D * COLS,
            bytes_accessed=slots * D * D * 4,
            transcendentals=0,
        ),
    )(*operands)


def after(parts, others):
    arrays, others = lax.optimization_barrier(([p[0] for p in parts], others))
    return [(array, p[1]) for array, p in zip(arrays, parts)], others


def orders():
    z, y = [zbits(e) for e in (0, 1, 3, 2)], [ybits(e) for e in (0, 1, 3, 2)]
    a4 = [e | xbits(i) for e in z for i in (0, 1)]
    b4 = [e | xbits(i) for e in y for i in (2, 3)]

    def both(i):
        return [m ^ y[i] for m in a4], [m ^ z[i] for m in b4]

    def other(parts):
        return [[m ^ CORE for m in p] for p in parts]

    near, sides, far = [*both(0)], [*both(1), *both(2)], [*both(3)]
    chunks = near + other(near) + sides + other(sides[:3]) + far + other(sides[3:] + far)
    return [m for p in chunks for m in p]


ORDER = orders()


def body(queries, keys, values, span_pos):
    flat = lax.axis_index("blk") * 2 + lax.axis_index("head")
    x = ((flat >> 2) & 1) * 2 + (flat & 1)

    by_head = jnp.stack(
        [
            keys.reshape(D, HEADS, D).transpose(1, 0, 2),
            values.reshape(D, HEADS, D).transpose(1, 2, 0),
        ],
        axis=1,
    )

    def head_part(e):
        return lax.dynamic_index_in_dim(by_head, x ^ e, 0, keepdims=True)

    def query_part(e):
        return lax.dynamic_slice_in_dim(queries, (x ^ e) * COLS, COLS, 1)

    shard = [head_part(0)] + [swap(head_part(e), xbits(e)) for e in (1, 2, 3)]
    q_parts = [query_part(0)] + [swap(query_part(e), xbits(e)) for e in (1, 2, 3)]
    own = jnp.concatenate(shard, 0)
    z1, z3, y1, y3 = zbits(1), zbits(3), ybits(1), ybits(3)
    pair_a, pair_b = (own[:2], [0, 1]), (own[2:], [xbits(2), xbits(3)])

    def moved(part, mask):
        return swap(part[0], mask), [m ^ mask for m in part[1]]

    def joined(p, q):
        return jnp.concatenate([p[0], q[0]], 0), p[1] + q[1]

    a2, b2 = joined(pair_a, moved(pair_a, z1)), joined(pair_b, moved(pair_b, y1))
    a4, b4 = joined(a2, moved(a2, z3)), joined(b2, moved(b2, y3))
    (a4, b4), q_parts = after((a4, b4), q_parts)
    sides = [moved(a4, y1), moved(b4, z1), moved(a4, y3), moved(b4, z3)]
    near = [a4, b4]
    near_other = [moved(p, CORE) for p in near]

    all_pos = span_pos[flat ^ jnp.array(ORDER, jnp.int32)]
    q_pos = span_pos[flat ^ jnp.array([xbits(e) for e in range(4)], jnp.int32)]
    before = []

    def run(chunk, state, blocks=()):
        at = len(before) * 8
        masks = [m for p in chunk for m in p[1]]
        assert list(ORDER[at : at + len(masks)]) == masks
        pos = all_pos[at : at + len(masks)]
        rank = jnp.sum((pos[None, :] < pos[:, None]).astype(jnp.int32), axis=1)
        count = jnp.sum((pos[None, :] < q_pos[:, None]).astype(jnp.int32), axis=1)
        arrays = [p[0] for p in chunk]
        out = attend(rank, count, all_pos, q_pos, q_parts, own, state, before, arrays, blocks)
        if not blocks:
            before.extend(arrays)
        return out

    state = run(near + near_other, None)
    sides, state = after(sides, state)
    sides_other = [moved(p, CORE) for p in sides[:3]]
    far = [moved(sides[0], y3), moved(sides[1], z3)]
    state = run(sides, state)
    (*far, late), state = after(far + [sides[3]], state)
    far_other = [moved(p, CORE) for p in [late] + far]
    state = run(sides_other + far[:1], state)
    last = far[1:] + far_other
    (far_out,) = run(last, state, (2,))
    pieces = [None, None, swap(far_out, xbits(2)), None]
    outs = run(last, state, (0, 1, 3))
    outs, pieces[2] = lax.optimization_barrier((outs, pieces[2]))
    pieces[0] = outs[0]
    pieces[1] = swap(outs[1], xbits(1))
    pieces[3] = swap(outs[2], xbits(3))
    result = jnp.zeros((D, HEADS * COLS), BF16)
    for e in range(4):
        result = lax.dynamic_update_slice(result, pieces[e], (0, (x ^ e) * COLS))
    return result


def solution(mesh):
    return jax.shard_map(
        body,
        mesh=mesh,
        in_specs=(P(AXES, None), P(AXES, None), P(AXES, None), P()),
        out_specs=P(AXES, None),
        check_vma=False,
    )
```

```python
import functools

import jax
import jax.numpy as jnp
from jax import lax
from jax.experimental import pallas as pl
from jax.experimental.pallas import tpu as pltpu
from jax.sharding import PartitionSpec as P

D = 128
HEADS = 4
GROUP = 8
COLS = GROUP * D
F32 = jnp.float32
BF16 = jnp.bfloat16
FACTOR = 1.4426950408889634 / D**0.5
SMALL = 4
LIMIT = 2.0**100
ONES = 16
ROWS = D + ONES
VMEM_LIMIT = 40 << 20
AXES = ("blk", "head")
TILE = 8


def xbits(e):
    return ((e >> 1) << 2) | (e & 1)


def zbits(e):
    return e << 5


def ybits(e):
    return e << 3


CORE = 2


def swap(array, mask):
    return lax.ppermute(array, AXES, [(i, i ^ mask) for i in range(128)])


def nt(a, b):
    return lax.dot_general(a, b, (((1,), (1,)), ((), ())), preferred_element_type=F32)


def nn(a, b):
    return lax.dot_general(a, b, (((1,), (0,)), ((), ())), preferred_element_type=F32)


def pick(choices, i):
    chosen = jnp.int32(choices[-1])
    for at, choice in reversed(list(enumerate(choices[:-1]))):
        chosen = jnp.where(i == at, choice, chosen)
    return chosen


def causal():
    row = lax.broadcasted_iota(jnp.int32, (D, COLS), 0)
    col = lax.broadcasted_iota(jnp.int32, (D, COLS), 1) % D
    return row <= col


def kernel(first, blocks, chunk_arrays, rank_ref, count_ref, all_pos_ref, q_pos_ref, *refs):
    refs = list(refs)
    q_refs = [refs.pop(0) for _ in range(4)]
    own = refs.pop(0) if first else None
    if not first:
        acc_in, shift_in = refs.pop(0), refs.pop(0)
    n_out = len(blocks) or 2
    arrays = [refs.pop(0) for _ in range(len(refs) - n_out - (9 if blocks else 5))]
    here = arrays[-chunk_arrays:]
    outs = [refs.pop(0) for _ in range(n_out)]
    keys, values, q_all, sem_k, sem_v = [refs.pop(0) for _ in range(5)]
    acc, shift = (refs.pop(0), refs.pop(0)) if blocks else outs
    todo = blocks or (0, 1, 2, 3)

    at = 0
    for array in here:

        def place(i, _, array=array, at=at):
            base = pl.multiple_of(rank_ref[at + i] * D, D)
            pltpu.make_async_copy(array.at[i, 0], keys.at[pl.ds(base, D), :], sem_k).start()
            pltpu.make_async_copy(
                array.at[i, 1], values.at[0:D, pl.ds(base, D)], sem_v
            ).start()
            return 0

        lax.fori_loop(0, array.shape[0], place, 0, unroll=True)
        at += array.shape[0]

    values[D:, :] = jnp.ones((ONES, values.shape[1]), BF16)
    for b in todo:
        for h in range(GROUP):
            q_all[b, h * D : (h + 1) * D, :] = q_refs[b][:, h * D : (h + 1) * D]

    if first:

        def diagonal(b, _):
            s = nt(own[b, 0], q_all[b]) * FACTOR
            s = jnp.where(causal(), s, -jnp.inf)
            m = jnp.max(s, axis=0, keepdims=True)
            p = jnp.exp2(s - m).astype(BF16)
            shift[b] = jnp.broadcast_to(m, (8, COLS))
            acc[b] = nn(jnp.concatenate([own[b, 1], jnp.ones((ONES, D), BF16)], axis=0), p)
            return 0

        lax.fori_loop(0, 4, diagonal, 0)
    else:
        for b in todo:
            acc[b] = acc_in[b]
            shift[b] = shift_in[b]

    pltpu.make_async_copy(keys, keys, sem_k).wait()
    pltpu.make_async_copy(values.at[0:D, :], values.at[0:D, :], sem_v).wait()

    def tile(b, at, width):
        size = width * D
        base = pl.multiple_of(at * D, SMALL * D)
        s = nt(keys[pl.ds(base, size), :], q_all[b])
        p = jnp.exp2(s * FACTOR - shift[b, 0:1, :]).astype(BF16)
        col = lax.broadcasted_iota(jnp.int32, (ROWS, size), 1)
        v = values[:, pl.ds(base, size)]
        v = jnp.where(col < (count_ref[b] - at) * D, v, jnp.zeros_like(v))
        acc[b] += nn(v, p)

    def block(b, _):
        count = count_ref[b]
        large = (count + TILE - 1 - SMALL) // TILE

        def step(j, _):
            tile(b, j * TILE, TILE)
            return 0

        lax.fori_loop(0, large, step, 0)
        pl.when(count > large * TILE)(lambda: tile(b, large * TILE, SMALL))
        return 0

    lax.fori_loop(0, len(todo), lambda i, c: block(pick(todo, i), c), 0)

    if not blocks:
        return
    k_one, v_one = refs

    def redo(b):
        q_pos = q_pos_ref[b]
        acc[b] = jnp.zeros((ROWS, COLS), F32)
        shift[b] = jnp.full((8, COLS), -jnp.inf, F32)

        def one(i, _):
            k_pos = all_pos_ref[i]

            @pl.when(k_pos <= q_pos)
            def _():
                at = 0
                for array in arrays:
                    n = array.shape[0]

                    @pl.when((i >= at) & (i < at + n))
                    def _(array=array, at=at):
                        pltpu.sync_copy(array.at[i - at, 0], k_one)
                        pltpu.sync_copy(array.at[i - at, 1], v_one.at[0:D, :])

                    at += n
                s = nt(k_one[...], q_all[b]) * FACTOR
                row = lax.broadcasted_iota(jnp.int32, (D, COLS), 0) + k_pos * D
                col = lax.broadcasted_iota(jnp.int32, (D, COLS), 1) % D + q_pos * D
                s = jnp.where(row <= col, s, -jnp.inf)
                old = shift[b, 0:1, :]
                m = jnp.maximum(old, jnp.max(s, axis=0, keepdims=True))
                safe = jnp.where(m == -jnp.inf, 0.0, m)
                p = jnp.exp2(s - safe).astype(BF16)
                shift[b] = jnp.broadcast_to(m, (8, COLS))
                acc[b] = acc[b] * jnp.exp2(old - safe) + nn(v_one[...], p)

            return 0

        lax.fori_loop(0, all_pos_ref.shape[0], one, 0)

    v_one[D:, :] = jnp.ones((ONES, D), BF16)

    def check(b, _):
        total = acc[b, D : D + 1, :]
        bad = jnp.max(jnp.where(total < LIMIT, 0.0, 1.0)) > 0.0
        pl.when(bad)(lambda: redo(b))
        return 0

    lax.fori_loop(0, len(todo), lambda i, c: check(pick(todo, i), c), 0)
    for o_ref, b in zip(outs, blocks):
        out = acc[b, :D, :] / acc[b, D : D + 1, :]
        for h in range(GROUP):
            o_ref[:, h * D : (h + 1) * D] = out[:, h * D : (h + 1) * D].T.astype(BF16)


def attend(rank, count, all_pos, q_pos, q_parts, own, state, before, here, blocks):
    first = state is None
    slots = sum(a.shape[0] for a in here)
    vmem = pl.BlockSpec(memory_space=pltpu.VMEM)
    smem = pl.BlockSpec(memory_space=pltpu.SMEM)
    hbm = pl.BlockSpec(memory_space=pl.ANY)
    arrays = (list(before) if blocks else []) + list(here)
    operands = [rank, count, all_pos, q_pos, *q_parts]
    specs = [smem] * 4 + [vmem] * 4
    operands += [own] if first else list(state)
    specs += [vmem] * (1 if first else 2)
    operands += arrays
    specs += [hbm] * len(arrays)
    scratch = [
        pltpu.VMEM((slots * D, D), BF16),
        pltpu.VMEM((ROWS, slots * D), BF16),
        pltpu.VMEM((4, COLS, D), BF16),
        pltpu.SemaphoreType.DMA,
        pltpu.SemaphoreType.DMA,
    ]
    if blocks:
        out_shape = [jax.ShapeDtypeStruct((D, COLS), BF16) for _ in blocks]
        scratch += [pltpu.VMEM((4, ROWS, COLS), F32), pltpu.VMEM((4, 8, COLS), F32)]
        scratch += [pltpu.VMEM((D, D), BF16), pltpu.VMEM((ROWS, D), BF16)]
    else:
        out_shape = [
            jax.ShapeDtypeStruct((4, ROWS, COLS), F32),
            jax.ShapeDtypeStruct((4, 8, COLS), F32),
        ]
    share = len(blocks) / 4 if blocks else 1
    return pl.pallas_call(
        functools.partial(kernel, first, tuple(blocks), len(here)),
        out_shape=out_shape,
        in_specs=specs,
        out_specs=[vmem] * len(out_shape),
        scratch_shapes=scratch,
        compiler_params=pltpu.CompilerParams(vmem_limit_bytes=VMEM_LIMIT),
        cost_estimate=pl.CostEstimate(
            flops=int(slots * 2 * share) * 8 * D * D * COLS,
            bytes_accessed=slots * D * D * 4,
            transcendentals=0,
        ),
    )(*operands)


def split_kernel(x_ref, k_ref, v_ref, *outs):
    for e, out in enumerate(outs):
        base = pl.multiple_of((x_ref[0] ^ e) * D, D)
        out[0, 0] = k_ref[:, pl.ds(base, D)]
        out[0, 1] = v_ref[:, pl.ds(base, D)].T


def split(x, keys, values):
    vmem = pl.BlockSpec(memory_space=pltpu.VMEM)
    return pl.pallas_call(
        split_kernel,
        out_shape=[jax.ShapeDtypeStruct((1, 2, D, D), BF16)] * HEADS,
        in_specs=[pl.BlockSpec(memory_space=pltpu.SMEM), vmem, vmem],
        out_specs=[vmem] * HEADS,
    )(x.reshape(1), keys, values)


def after(parts, others):
    arrays, others = lax.optimization_barrier(([p[0] for p in parts], others))
    return [(array, p[1]) for array, p in zip(arrays, parts)], others


def orders():
    z, y = [zbits(e) for e in (0, 1, 3, 2)], [ybits(e) for e in (0, 1, 3, 2)]
    a4 = [e | xbits(i) for e in z for i in (0, 1)]
    b4 = [e | xbits(i) for e in y for i in (2, 3)]

    def both(i):
        return [m ^ y[i] for m in a4], [m ^ z[i] for m in b4]

    def other(parts):
        return [[m ^ CORE for m in p] for p in parts]

    near, sides, far = [*both(0)], [*both(1), *both(2)], [*both(3)]
    chunks = near + other(near) + sides + other(sides[:3]) + far + other(sides[3:] + far)
    return [m for p in chunks for m in p]


ORDER = orders()


def body(queries, keys, values, span_pos):
    flat = lax.axis_index("blk") * 2 + lax.axis_index("head")
    x = ((flat >> 2) & 1) * 2 + (flat & 1)

    heads = split(x, keys, values)

    def query_part(e):
        return lax.dynamic_slice_in_dim(queries, (x ^ e) * COLS, COLS, 1)

    shard = [heads[0]] + [swap(heads[e], xbits(e)) for e in (1, 2, 3)]
    q_parts = [query_part(0)] + [swap(query_part(e), xbits(e)) for e in (1, 2, 3)]
    own = jnp.concatenate(shard, 0)
    z1, z3, y1, y3 = zbits(1), zbits(3), ybits(1), ybits(3)
    pair_a, pair_b = (own[:2], [0, 1]), (own[2:], [xbits(2), xbits(3)])

    def moved(part, mask):
        return swap(part[0], mask), [m ^ mask for m in part[1]]

    def joined(p, q):
        return jnp.concatenate([p[0], q[0]], 0), p[1] + q[1]

    a2, b2 = joined(pair_a, moved(pair_a, z1)), joined(pair_b, moved(pair_b, y1))
    a4, b4 = joined(a2, moved(a2, z3)), joined(b2, moved(b2, y3))
    (a4, b4), q_parts = after((a4, b4), q_parts)
    sides = [moved(a4, y1), moved(b4, z1), moved(a4, y3), moved(b4, z3)]
    near = [a4, b4]
    near_other = [moved(p, CORE) for p in near]

    all_pos = span_pos[flat ^ jnp.array(ORDER, jnp.int32)]
    q_pos = span_pos[flat ^ jnp.array([xbits(e) for e in range(4)], jnp.int32)]
    before = []

    def run(chunk, state, blocks=()):
        at = len(before) * 8
        masks = [m for p in chunk for m in p[1]]
        assert list(ORDER[at : at + len(masks)]) == masks
        pos = all_pos[at : at + len(masks)]
        rank = jnp.sum((pos[None, :] < pos[:, None]).astype(jnp.int32), axis=1)
        count = jnp.sum((pos[None, :] < q_pos[:, None]).astype(jnp.int32), axis=1)
        arrays = [p[0] for p in chunk]
        out = attend(rank, count, all_pos, q_pos, q_parts, own, state, before, arrays, blocks)
        if not blocks:
            before.extend(arrays)
        return out

    state = run(near + near_other, None)
    sides, state = after(sides, state)
    sides_other = [moved(p, CORE) for p in sides[:3]]
    far = [moved(sides[0], y3), moved(sides[1], z3)]
    state = run(sides, state)
    (*far, late), state = after(far + [sides[3]], state)
    far_other = [moved(p, CORE) for p in [late] + far]
    state = run(sides_other + far[:1], state)
    last = far[1:] + far_other
    (far_out,) = run(last, state, (2,))
    pieces = [None, None, swap(far_out, xbits(2)), None]
    outs = run(last, state, (1, 3))
    pieces[1], pieces[3] = swap(outs[0], xbits(1)), swap(outs[1], xbits(3))
    state, pieces[2] = lax.optimization_barrier((state, pieces[2]))
    (pieces[0],) = run(last, state, (0,))
    result = jnp.zeros((D, HEADS * COLS), BF16)
    for e in range(4):
        result = lax.dynamic_update_slice(result, pieces[e], (0, (x ^ e) * COLS))
    return result


def solution(mesh):
    return jax.shard_map(
        body,
        mesh=mesh,
        in_specs=(P(AXES, None), P(AXES, None), P(AXES, None), P()),
        out_specs=P(AXES, None),
        check_vma=False,
    )
```

```python
import functools

import jax
import jax.numpy as jnp
from jax import lax
from jax.experimental import pallas as pl
from jax.experimental.pallas import tpu as pltpu
from jax.sharding import PartitionSpec as P

D = 128
HEADS = 4
GROUP = 8
COLS = GROUP * D
F32 = jnp.float32
BF16 = jnp.bfloat16
FACTOR = 1.4426950408889634 / D**0.5
SMALL = 4
LIMIT = 2.0**100
ONES = 16
ROWS = D + ONES
VMEM_LIMIT = 40 << 20
AXES = ("blk", "head")
TILE = 8


def xbits(e):
    return ((e >> 1) << 2) | (e & 1)


def zbits(e):
    return e << 5


def ybits(e):
    return e << 3


CORE = 2


def swap(array, mask):
    return lax.ppermute(array, AXES, [(i, i ^ mask) for i in range(128)])


def nt(a, b):
    return lax.dot_general(a, b, (((1,), (1,)), ((), ())), preferred_element_type=F32)


def nn(a, b):
    return lax.dot_general(a, b, (((1,), (0,)), ((), ())), preferred_element_type=F32)


def pick(choices, i):
    chosen = jnp.int32(choices[-1])
    for at, choice in reversed(list(enumerate(choices[:-1]))):
        chosen = jnp.where(i == at, choice, chosen)
    return chosen


def causal():
    row = lax.broadcasted_iota(jnp.int32, (D, COLS), 0)
    col = lax.broadcasted_iota(jnp.int32, (D, COLS), 1) % D
    return row <= col


def kernel(first, blocks, chunk_arrays, rank_ref, count_ref, all_pos_ref, q_pos_ref, *refs):
    refs = list(refs)
    todo = blocks or (0, 1, 2, 3)
    q_refs = {b: refs.pop(0) for b in todo}
    own = refs.pop(0) if first else None
    if not first:
        acc_in, shift_in = refs.pop(0), refs.pop(0)
    n_out = len(blocks) or 2
    arrays = [refs.pop(0) for _ in range(len(refs) - n_out - (9 if blocks else 5))]
    here = arrays[-chunk_arrays:]
    outs = [refs.pop(0) for _ in range(n_out)]
    keys, values, q_all, sem_k, sem_v = [refs.pop(0) for _ in range(5)]
    acc, shift = (refs.pop(0), refs.pop(0)) if blocks else outs

    at = 0
    for array in here:

        def place(i, _, array=array, at=at):
            base = pl.multiple_of(rank_ref[at + i] * D, D)
            pltpu.make_async_copy(array.at[i, 0], keys.at[pl.ds(base, D), :], sem_k).start()
            pltpu.make_async_copy(
                array.at[i, 1], values.at[0:D, pl.ds(base, D)], sem_v
            ).start()
            return 0

        lax.fori_loop(0, array.shape[0], place, 0, unroll=True)
        at += array.shape[0]

    values[D:, :] = jnp.ones((ONES, values.shape[1]), BF16)
    for b in todo:
        for h in range(GROUP):
            q_all[b, h * D : (h + 1) * D, :] = q_refs[b][:, h * D : (h + 1) * D]

    if first:

        def diagonal(b, _):
            s = nt(own[b, 0], q_all[b]) * FACTOR
            s = jnp.where(causal(), s, -jnp.inf)
            m = jnp.max(s, axis=0, keepdims=True)
            p = jnp.exp2(s - m).astype(BF16)
            shift[b] = jnp.broadcast_to(m, (8, COLS))
            acc[b] = nn(jnp.concatenate([own[b, 1], jnp.ones((ONES, D), BF16)], axis=0), p)
            return 0

        lax.fori_loop(0, 4, diagonal, 0)
    else:
        for b in todo:
            acc[b] = acc_in[b]
            shift[b] = shift_in[b]

    pltpu.make_async_copy(keys, keys, sem_k).wait()
    pltpu.make_async_copy(values.at[0:D, :], values.at[0:D, :], sem_v).wait()

    def tile(b, at, width):
        size = width * D
        base = pl.multiple_of(at * D, SMALL * D)
        s = nt(keys[pl.ds(base, size), :], q_all[b])
        p = jnp.exp2(s * FACTOR - shift[b, 0:1, :]).astype(BF16)
        col = lax.broadcasted_iota(jnp.int32, (ROWS, size), 1)
        v = values[:, pl.ds(base, size)]
        v = jnp.where(col < (count_ref[b] - at) * D, v, jnp.zeros_like(v))
        acc[b] += nn(v, p)

    def block(b, _):
        count = count_ref[b]
        large = (count + TILE - 1 - SMALL) // TILE

        def step(j, _):
            tile(b, j * TILE, TILE)
            return 0

        lax.fori_loop(0, large, step, 0)
        pl.when(count > large * TILE)(lambda: tile(b, large * TILE, SMALL))
        return 0

    lax.fori_loop(0, len(todo), lambda i, c: block(pick(todo, i), c), 0)

    if not blocks:
        return
    k_one, v_one = refs

    def redo(b):
        q_pos = q_pos_ref[b]
        acc[b] = jnp.zeros((ROWS, COLS), F32)
        shift[b] = jnp.full((8, COLS), -jnp.inf, F32)

        def one(i, _):
            k_pos = all_pos_ref[i]

            @pl.when(k_pos <= q_pos)
            def _():
                at = 0
                for array in arrays:
                    n = array.shape[0]

                    @pl.when((i >= at) & (i < at + n))
                    def _(array=array, at=at):
                        pltpu.sync_copy(array.at[i - at, 0], k_one)
                        pltpu.sync_copy(array.at[i - at, 1], v_one.at[0:D, :])

                    at += n
                s = nt(k_one[...], q_all[b]) * FACTOR
                row = lax.broadcasted_iota(jnp.int32, (D, COLS), 0) + k_pos * D
                col = lax.broadcasted_iota(jnp.int32, (D, COLS), 1) % D + q_pos * D
                s = jnp.where(row <= col, s, -jnp.inf)
                old = shift[b, 0:1, :]
                m = jnp.maximum(old, jnp.max(s, axis=0, keepdims=True))
                safe = jnp.where(m == -jnp.inf, 0.0, m)
                p = jnp.exp2(s - safe).astype(BF16)
                shift[b] = jnp.broadcast_to(m, (8, COLS))
                acc[b] = acc[b] * jnp.exp2(old - safe) + nn(v_one[...], p)

            return 0

        lax.fori_loop(0, all_pos_ref.shape[0], one, 0)

    v_one[D:, :] = jnp.ones((ONES, D), BF16)

    def check(b, _):
        total = acc[b, D : D + 1, :]
        bad = jnp.max(jnp.where(total < LIMIT, 0.0, 1.0)) > 0.0
        pl.when(bad)(lambda: redo(b))
        return 0

    lax.fori_loop(0, len(todo), lambda i, c: check(pick(todo, i), c), 0)
    for o_ref, b in zip(outs, blocks):
        out = acc[b, :D, :] / acc[b, D : D + 1, :]
        for h in range(GROUP):
            o_ref[:, h * D : (h + 1) * D] = out[:, h * D : (h + 1) * D].T.astype(BF16)


def attend(rank, count, all_pos, q_pos, q_parts, own, state, before, here, blocks):
    first = state is None
    slots = sum(a.shape[0] for a in here)
    vmem = pl.BlockSpec(memory_space=pltpu.VMEM)
    smem = pl.BlockSpec(memory_space=pltpu.SMEM)
    hbm = pl.BlockSpec(memory_space=pl.ANY)
    arrays = (list(before) if blocks else []) + list(here)
    q_parts = [q_parts[b] for b in blocks or range(4)]
    operands = [rank, count, all_pos, q_pos, *q_parts]
    specs = [smem] * 4 + [vmem] * len(q_parts)
    operands += [own] if first else list(state)
    specs += [vmem] * (1 if first else 2)
    operands += arrays
    specs += [hbm] * len(arrays)
    scratch = [
        pltpu.VMEM((slots * D, D), BF16),
        pltpu.VMEM((ROWS, slots * D), BF16),
        pltpu.VMEM((4, COLS, D), BF16),
        pltpu.SemaphoreType.DMA,
        pltpu.SemaphoreType.DMA,
    ]
    if blocks:
        out_shape = [jax.ShapeDtypeStruct((D, COLS), BF16) for _ in blocks]
        scratch += [pltpu.VMEM((4, ROWS, COLS), F32), pltpu.VMEM((4, 8, COLS), F32)]
        scratch += [pltpu.VMEM((D, D), BF16), pltpu.VMEM((ROWS, D), BF16)]
    else:
        out_shape = [
            jax.ShapeDtypeStruct((4, ROWS, COLS), F32),
            jax.ShapeDtypeStruct((4, 8, COLS), F32),
        ]
    share = len(blocks) / 4 if blocks else 1
    return pl.pallas_call(
        functools.partial(kernel, first, tuple(blocks), len(here)),
        out_shape=out_shape,
        in_specs=specs,
        out_specs=[vmem] * len(out_shape),
        scratch_shapes=scratch,
        compiler_params=pltpu.CompilerParams(vmem_limit_bytes=VMEM_LIMIT),
        cost_estimate=pl.CostEstimate(
            flops=int(slots * 2 * share) * 8 * D * D * COLS,
            bytes_accessed=slots * D * D * 4,
            transcendentals=0,
        ),
    )(*operands)


def split_kernel(x_ref, k_ref, v_ref, *outs):
    for e, out in enumerate(outs):
        base = pl.multiple_of((x_ref[0] ^ e) * D, D)
        out[0, 0] = k_ref[:, pl.ds(base, D)]
        out[0, 1] = v_ref[:, pl.ds(base, D)].T


def split(x, keys, values):
    vmem = pl.BlockSpec(memory_space=pltpu.VMEM)
    return pl.pallas_call(
        split_kernel,
        out_shape=[jax.ShapeDtypeStruct((1, 2, D, D), BF16)] * HEADS,
        in_specs=[pl.BlockSpec(memory_space=pltpu.SMEM), vmem, vmem],
        out_specs=[vmem] * HEADS,
    )(x.reshape(1), keys, values)


def after(parts, others):
    arrays, others = lax.optimization_barrier(([p[0] for p in parts], others))
    return [(array, p[1]) for array, p in zip(arrays, parts)], others


def orders():
    z, y = [zbits(e) for e in (0, 1, 3, 2)], [ybits(e) for e in (0, 1, 3, 2)]
    a4 = [e | xbits(i) for e in z for i in (0, 1)]
    b4 = [e | xbits(i) for e in y for i in (2, 3)]

    def both(i):
        return [m ^ y[i] for m in a4], [m ^ z[i] for m in b4]

    def other(parts):
        return [[m ^ CORE for m in p] for p in parts]

    near, sides, far = [*both(0)], [*both(1), *both(2)], [*both(3)]
    chunks = near + other(near) + sides + other(sides[:3]) + far + other(sides[3:] + far)
    return [m for p in chunks for m in p]


ORDER = orders()


def body(queries, keys, values, span_pos):
    flat = lax.axis_index("blk") * 2 + lax.axis_index("head")
    x = ((flat >> 2) & 1) * 2 + (flat & 1)

    heads = split(x, keys, values)

    def query_part(e):
        return lax.dynamic_slice_in_dim(queries, (x ^ e) * COLS, COLS, 1)

    shard = [heads[0]] + [swap(heads[e], xbits(e)) for e in (1, 2, 3)]
    q_parts = [query_part(0)] + [swap(query_part(e), xbits(e)) for e in (1, 2, 3)]
    own = jnp.concatenate(shard, 0)
    z1, z3, y1, y3 = zbits(1), zbits(3), ybits(1), ybits(3)
    pair_a, pair_b = (own[:2], [0, 1]), (own[2:], [xbits(2), xbits(3)])

    def moved(part, mask):
        return swap(part[0], mask), [m ^ mask for m in part[1]]

    def joined(p, q):
        return jnp.concatenate([p[0], q[0]], 0), p[1] + q[1]

    a2, b2 = joined(pair_a, moved(pair_a, z1)), joined(pair_b, moved(pair_b, y1))
    a4, b4 = joined(a2, moved(a2, z3)), joined(b2, moved(b2, y3))
    (a4, b4), q_parts = after((a4, b4), q_parts)
    sides = [moved(a4, y1), moved(b4, z1), moved(a4, y3), moved(b4, z3)]
    near = [a4, b4]
    near_other = [moved(p, CORE) for p in near]

    all_pos = span_pos[flat ^ jnp.array(ORDER, jnp.int32)]
    q_pos = span_pos[flat ^ jnp.array([xbits(e) for e in range(4)], jnp.int32)]
    before = []

    def run(chunk, state, blocks=()):
        at = len(before) * 8
        masks = [m for p in chunk for m in p[1]]
        assert list(ORDER[at : at + len(masks)]) == masks
        pos = all_pos[at : at + len(masks)]
        rank = jnp.sum((pos[None, :] < pos[:, None]).astype(jnp.int32), axis=1)
        count = jnp.sum((pos[None, :] < q_pos[:, None]).astype(jnp.int32), axis=1)
        arrays = [p[0] for p in chunk]
        out = attend(rank, count, all_pos, q_pos, q_parts, own, state, before, arrays, blocks)
        if not blocks:
            before.extend(arrays)
        return out

    state = run(near + near_other, None)
    sides, state = after(sides, state)
    sides_other = [moved(p, CORE) for p in sides[:3]]
    far = [moved(sides[0], y3), moved(sides[1], z3)]
    state = run(sides, state)
    (*far, late), state = after(far + [sides[3]], state)
    far_other = [moved(p, CORE) for p in [late] + far]
    state = run(sides_other + far[:1], state)
    last = far[1:] + far_other
    (far_out,) = run(last, state, (2,))
    pieces = [None, None, swap(far_out, xbits(2)), None]
    outs = run(last, state, (1, 3))
    pieces[1], pieces[3] = swap(outs[0], xbits(1)), swap(outs[1], xbits(3))
    state, pieces[2] = lax.optimization_barrier((state, pieces[2]))
    (pieces[0],) = run(last, state, (0,))
    result = jnp.zeros((D, HEADS * COLS), BF16)
    for e in range(4):
        result = lax.dynamic_update_slice(result, pieces[e], (0, (x ^ e) * COLS))
    return result


def solution(mesh):
    return jax.shard_map(
        body,
        mesh=mesh,
        in_specs=(P(AXES, None), P(AXES, None), P(AXES, None), P()),
        out_specs=P(AXES, None),
        check_vma=False,
    )
```
